1024 devices in a mesh: dp: 64 (over z, core), et: 16 (over y, x).
Axes of the slice: x: 4, y: 4, z: 32, core: 2. Of those that a mesh axis runs over, the one named last changes fastest.
Arguments:
- pre_gate: bfloat16 [16384, 5376], P('dp', 'et'), may hold values from -6 to 6
- pre_up: bfloat16 [16384, 5376], P('dp', 'et'), may hold values from -6 to 6
- down_weight: bfloat16 [5376, 6144], P('et'), may hold values from -0.078125 to 0.078125
- row_token: int32 [16384], P('dp'), may hold values from 0 to 384, as said below
- block_count: int32 [64], P('dp'), may hold values from 1 to 2, as said below
- router_logits: float32 [24576, 16], P('dp'), as said below
- tokens_in: bfloat16 [24576, 6144], P('dp', 'et'), may hold values from -6 to 6
- out_grad: bfloat16 [24576, 6144], P('dp', 'et'), may hold values from -12 to 12
Outputs:
- combined: bfloat16 [24576, 6144], P('dp', 'et')
- grad_gate: bfloat16 [16384, 5376], P('dp', 'et')
- grad_up: bfloat16 [16384, 5376], P('dp', 'et')
- router_grad: float32 [16, 6144], P(None, 'et')
The draws below stay inside these ranges and needn't reach their ends.
Inputs may be any that keep to these rules, and one draw needn't show every extreme that they name: `row_token`: within the 256 slots of one index of dp, the first r slots hold distinct tokens below 384 and the other slots hold 384, with r between 64 and 256; r = 256 on at least one index of dp. `block_count`: the number of blocks of 128 slots that hold r's live slots, rounded up, on each index of dp. `router_logits`: finite router scores.
All inputs are finite; a program needn't handle non-finite values.
Results may differ from the reference program's by a relative error of at most 0.0051.
Values may be sent and summed in bfloat16 or wider, within the bound.
A program may use at most 64 MiB of HBM per device.

```python
import jax
import jax.numpy as jnp
from jax import lax

D = 6144
FF = 5376
EXPERTS = 16
BLOCK = 128
TOK_DEV = 384
CAP = 256
TOKENS = 24576
N_DP = 64


def slot_layout(key):
    first_key, second_key, third_key, fourth_key = jax.random.split(key, 4)
    counts = jax.random.randint(first_key, (N_DP,), CAP // 4, CAP + 1)
    fullest = jax.random.randint(second_key, (), 0, N_DP)
    filled = jax.random.randint(fourth_key, (N_DP,), 0, 2) == 1
    counts = jnp.where((jnp.arange(N_DP) == fullest) | filled, CAP, counts)
    orders = jax.vmap(lambda sub_key: jax.random.permutation(sub_key, TOK_DEV))(jax.random.split(third_key, N_DP))[:, :CAP]
    slot_ids = jnp.arange(CAP)
    tokens = jnp.where(slot_ids[None, :] < counts[:, None], orders, TOK_DEV)
    return (counts.astype(jnp.int32), tokens.reshape(-1).astype(jnp.int32))


def draw_row_token(key, part):
    layout = slot_layout(key)
    return layout[1]


def draw_block_count(key, part):
    layout = slot_layout(key)
    return ((layout[0] + BLOCK - 1) // BLOCK).astype(jnp.int32)


def draw_router_logits(key, part):
    key = jax.random.fold_in(key, 7)
    first_key = jax.random.fold_in(key, 0)
    fourth_key = jax.random.fold_in(key, 3)
    expert_ids = jnp.arange(EXPERTS)[None, :]
    leading = jax.random.uniform(fourth_key, (TOKENS, 1), jnp.float32, 2.0, 4.5)
    others = jax.random.normal(first_key, (TOKENS, EXPERTS), jnp.float32)
    return jnp.where(expert_ids == 0, leading, others)


def level_of(rng, shape, pieces, smallest, top_value):
    def one(axis_at, shards_of):
        steps = jax.random.uniform(jax.random.fold_in(jax.random.fold_in(rng, 6), axis_at), (shards_of,), jnp.float32, smallest / len(pieces), top_value / len(pieces))
        return jnp.repeat(jnp.exp(steps), shape[axis_at] // shards_of).reshape((-1,) + (1,) * (len(shape) - axis_at - 1))

    loudness = one(*pieces[0])
    for cut in pieces[1:]:
        loudness = loudness * one(*cut)
    return loudness


def normal_values(key, shape, deviation, bound, shards=(), held_as=jnp.bfloat16):
    loudness = level_of(key, shape, shards, -0.22, 0.18) if shards else 1.0
    array = jax.random.normal(key, shape, jnp.float32) * deviation * loudness
    return jnp.minimum(jnp.maximum(array, -bound), bound).astype(held_as)


def setup_inputs(seed: int = 0) -> dict:
    keys = jax.random.split(jax.random.key(seed), 9)
    pre_gate = normal_values(keys[0], (N_DP * CAP, FF), 1.0, 6.0, ((0, 64), (1, 16)))
    pre_up = normal_values(keys[1], (N_DP * CAP, FF), 1.0, 6.0, ((0, 64), (1, 16)))
    down_weight = normal_values(keys[2], (FF, D), FF ** -0.5, 0.078125, ((0, 16),))
    row_token = draw_row_token(jax.random.fold_in(keys[8], 71), 0)
    block_count = draw_block_count(jax.random.fold_in(keys[8], 71), 0)
    router_logits = draw_router_logits(jax.random.fold_in(keys[8], 71), 0)
    tokens_in = normal_values(keys[6], (TOKENS, D), 1.0, 6.0, ((0, 64), (1, 16)))
    out_grad = normal_values(keys[7], (TOKENS, D), 2.0, 12.0, ((0, 64), (1, 16)))
    return dict(pre_gate=pre_gate, pre_up=pre_up, down_weight=down_weight, row_token=row_token, block_count=block_count, router_logits=router_logits, tokens_in=tokens_in, out_grad=out_grad)


def reference(pre_gate, pre_up, down_weight, row_token, block_count, router_logits, tokens_in, out_grad):
    slot_total = N_DP * CAP
    slot_ids = jnp.arange(slot_total, dtype=jnp.int32)
    device_ids = slot_ids // CAP
    live_slot = ((slot_ids % CAP) // BLOCK < block_count[device_ids]) & (row_token < TOK_DEV)
    global_index = jnp.where(live_slot, device_ids * TOK_DEV + row_token, TOKENS).astype(jnp.int32)
    safe_index = jnp.minimum(global_index, TOKENS - 1)
    router_probs = jax.nn.softmax(router_logits.astype(jnp.float32), axis=-1)
    first_prob = router_probs[:, 0]
    row_prob = jnp.where(live_slot, first_prob[safe_index], 0.0)
    gate_value = pre_gate.astype(jnp.float32)
    up_value = pre_up.astype(jnp.float32)
    sigmoid_gate = jax.nn.sigmoid(gate_value)
    hidden = jnp.where(live_slot[:, None], gate_value * sigmoid_gate * up_value, 0.0).astype(jnp.bfloat16)
    expert_out = jnp.dot(hidden, down_weight, preferred_element_type=jnp.float32)
    combined = jnp.zeros((TOKENS, D), jnp.float32).at[global_index].add(row_prob[:, None] * expert_out, mode="drop").astype(jnp.bfloat16)
    slot_grad = jnp.where(live_slot[:, None], out_grad[safe_index], 0.0).astype(jnp.bfloat16)
    weight_grad = jnp.sum(slot_grad.astype(jnp.float32) * expert_out, axis=1)
    raw_back = lax.dot_general(slot_grad, down_weight, (((1,), (1,)), ((), ())), preferred_element_type=jnp.float32)
    hidden_grad = row_prob[:, None] * raw_back
    grad_up = (hidden_grad * gate_value * sigmoid_gate).astype(jnp.bfloat16)
    grad_gate = (hidden_grad * up_value * sigmoid_gate * (1.0 + gate_value * (1.0 - sigmoid_gate))).astype(jnp.bfloat16)
    token_weight = jnp.zeros((TOKENS,), jnp.float32).at[global_index].add(weight_grad, mode="drop")
    one_hot = (jnp.arange(EXPERTS) == 0).astype(jnp.float32)
    logit_grad = (first_prob[:, None] * (one_hot[None, :] - router_probs) * token_weight[:, None]).astype(jnp.bfloat16)
    router_grad = jnp.dot(logit_grad.T, tokens_in, preferred_element_type=jnp.float32) * (TOKENS ** -0.5)
    return combined, grad_gate, grad_up, router_grad
```

```python
import functools

import jax
import jax.numpy as jnp
from jax import lax
from jax.experimental import pallas as pl
from jax.experimental.pallas import tpu as pltpu
from jax.sharding import PartitionSpec as P

BLOCK = 128
MESH = pl.DeviceIdType.MESH
RING = (1, 3, 2)
F32 = jnp.float32
BF16 = jnp.bfloat16


def kernel(
    nz,
    scale,
    rt_ref,
    bc_ref,
    lg_ref,
    g_ref,
    u_ref,
    w_hbm,
    t_ref,
    og_ref,
    comb_ref,
    gg_ref,
    gu_ref,
    rg_ref,
    wv,
    hid,
    lp,
    onehot,
    pm,
    ct,
    tslot,
    sg,
    raw,
    part,
    r1,
    p2,
    r2,
    wgb,
    rp,
    nearb,
    farb,
    rgb,
    w_sem,
    ag_ss,
    ag_rs,
    r1_ss,
    r1_rs,
    r2_ss,
    r2_rs,
    wg_ss,
    wg_rs,
    near_ss,
    near_rs,
    far_ss,
    far_rs,
    core_ss,
    core_rs,
):
    slots = g_ref.shape[0]
    half = slots // 2
    ff = g_ref.shape[1]
    ffp = hid.shape[1]
    toks, cols = og_ref.shape
    ngrp = nz // 2
    dp = lax.axis_index("dp")
    et = lax.axis_index("et")
    x, y, z, c = et % 4, et // 4, dp // 2, dp % 2
    zp, grp = z % 2, z // 2

    def et_at(yy, xx):
        return (yy % 4) * 4 + xx % 4

    def copy(src, dst, ss, rs, d_dp, d_et):
        return pltpu.make_async_remote_copy(
            src_ref=src, dst_ref=dst, send_sem=ss, recv_sem=rs, device_id=(d_dp, d_et), device_id_type=MESH
        )

    def arrived(ref, rs):
        copy(ref, ref, rs, rs, dp, et_at(y, x + 1)).wait_recv()

    def near_peer(k):
        return (grp * 2 + (zp + k // 2) % 2) * 2 + (c + k) % 2

    barrier = pltpu.get_barrier_semaphore()

    def greet(d_dp, d_et):
        pl.semaphore_signal(barrier, 1, device_id=(d_dp, d_et), device_id_type=MESH)

    def greet_far(k, carry):
        greet((((grp + k) % ngrp) * 2 + zp) * 2 + c, et)
        return carry

    def greet_et(k, carry):
        greet(dp, et_at(y + k // 4, x + k % 4))
        return carry

    lax.fori_loop(1, ngrp, greet_far, 0)
    lax.fori_loop(1, 16, greet_et, 0)
    for k in (1, 2, 3):
        greet(near_peer(k), et)

    w_copy = pltpu.make_async_copy(w_hbm, wv.at[pl.ds(0, ff)], w_sem)
    w_copy.start()

    row_tok = rt_ref[...]
    slot_block = lax.broadcasted_iota(jnp.int32, row_tok.shape, 1) // BLOCK
    row_tok = jnp.where((slot_block < bc_ref[0]) & (row_tok < toks), row_tok, toks).astype(F32)
    row_tok = jnp.broadcast_to(row_tok, (128, slots)).T
    for k in range(toks // 128):
        lane = lax.broadcasted_iota(jnp.int32, (slots, 128), 1).astype(F32) + float(k * 128)
        onehot[:, k * 128 : (k + 1) * 128] = jnp.where(row_tok == lane, 1.0, 0.0).astype(BF16)
    sg[et] = jnp.dot(onehot[...], og_ref[...], preferred_element_type=F32).astype(BF16)

    pl.semaphore_wait(barrier, ngrp - 1 + 15 + 3)

    sends = []

    def send(block, h, d_et):
        view = sg.at[block, pl.ds(h * half, half)]
        cp = copy(view, view, ag_ss.at[len(sends)], ag_rs.at[block * 2 + h], dp, d_et)
        cp.start()
        sends.append(cp)

    def wait_block(block, h):
        arrived(sg.at[block, pl.ds(h * half, half)], ag_rs.at[block * 2 + h])

    for d in RING:
        send(et, 0, et_at(y, x + d))
        send(et, 1, et_at(y + d, x))
    for d in RING:
        send(et, 0, et_at(y + d, x))
        send(et, 1, et_at(y, x + d))

    gate = g_ref[...].astype(F32)
    hid[:, ffp - 128 : ffp] = jnp.zeros((slots, 128), BF16)
    hid[:, 0:ff] = (gate * jax.nn.sigmoid(gate) * u_ref[...].astype(F32)).astype(BF16)
    wv[ff:ffp] = jnp.zeros((ffp - ff, wv.shape[1]), BF16)
    w_copy.wait()
    live_rows = row_tok < float(toks)

    hid[...] = jnp.where(jnp.concatenate([live_rows] * (ffp // 128), axis=1), hid[...], jnp.zeros((), BF16))

    def forward_block(j, carry):
        w_j = wv[:, pl.ds(pl.multiple_of(j * cols, 128), cols)]
        part[j] = jnp.dot(hid[...], w_j, preferred_element_type=F32).astype(BF16)
        return carry

    lax.fori_loop(0, 16, forward_block, 0)

    for d in RING:
        block = et_at(y, x + d)
        wait_block(block, 0)
        for e in RING:
            send(block, 0, et_at(y + e, x))
        block = et_at(y + d, x)
        wait_block(block, 1)
        for e in RING:
            send(block, 1, et_at(y, x + e))

    lp[...] = jnp.zeros(lp.shape, F32)
    lp[:, 0 : lg_ref.shape[1]] = lg_ref[...]
    lane = lax.broadcasted_iota(jnp.int32, lp.shape, 1)
    valid = lane < lg_ref.shape[1]
    logit = lp[...]
    top = jnp.max(jnp.where(valid, logit, -jnp.inf), axis=1, keepdims=True)
    ex = jnp.where(valid, jnp.exp(jnp.where(valid, logit - top, 0.0)), 0.0)
    probs = ex / jnp.sum(ex, axis=1, keepdims=True)
    p0 = probs[:, 0:1]
    coef = p0 * (jnp.where(lane == 0, 1.0, 0.0) - probs)
    table = jnp.where(valid, coef, jnp.where(lane == lg_ref.shape[1], p0, 0.0))
    hi = table.astype(BF16)
    rest = table - hi.astype(F32)
    mid = rest.astype(BF16)
    low = (rest - mid.astype(F32)).astype(BF16)
    pm[...] = (
        jnp.dot(onehot[...], low, preferred_element_type=F32)
        + jnp.dot(onehot[...], mid, preferred_element_type=F32)
        + jnp.dot(onehot[...], hi, preferred_element_type=F32)
    )
    ct[...] = pm[...].T
    tslot[...] = jnp.dot(onehot[...], t_ref[...], preferred_element_type=F32).astype(BF16)

    def back(block):
        w_j = wv[:, pl.ds(pl.multiple_of(block * cols, 128), cols)]
        return lax.dot_general(sg[block], w_j, (((1,), (1,)), ((), ())), preferred_element_type=F32)

    raw[...] = back(et)
    order = [(0, 1), (1, 0), (0, 3), (3, 0), (0, 2), (2, 0)]
    order += [(1, 1), (1, 3), (3, 1), (3, 3), (1, 2), (2, 1), (3, 2), (2, 3), (2, 2)]
    for dy, dx in order:
        block = et_at(y + dy, x + dx)
        if dx == 0:
            wait_block(block, 0)
        elif dy == 0:
            wait_block(block, 1)
        else:
            wait_block(block, 0)
            wait_block(block, 1)
        raw[...] += back(block)

    prod = hid[...].astype(F32) * raw[...]
    fold = prod[:, 0:128]
    for k in range(1, ffp // 128):
        fold = fold + prod[:, k * 128 : (k + 1) * 128]
    wgb[et] = jnp.sum(fold.T, axis=0, keepdims=True)

    def wg_copy(k):
        return copy(wgb.at[et], wgb.at[et], wg_ss.at[k], wg_rs.at[et], dp, et_at(y + k // 4, x + k % 4))

    def wg_send(k, carry):
        wg_copy(k).start()
        return carry

    lax.fori_loop(1, 16, wg_send, 0)

    first = []
    for far_off in (2, 1, 3, 0):
        for d in RING:
            yy, xx = (y + far_off) % 4, (x + d) % 4
            cp = copy(
                part.at[yy * 4 + xx, pl.ds(0, half)],
                r1.at[0, x, yy],
                r1_ss.at[len(first)],
                r1_rs.at[x * 4 + yy],
                dp,
                et_at(y, xx),
            )
            cp.start()
            first.append(cp)
            yy, xx = (y + d) % 4, (x + far_off) % 4
            cp = copy(
                part.at[yy * 4 + xx, pl.ds(half, half)],
                r1.at[1, y, xx],
                r1_ss.at[len(first)],
                r1_rs.at[16 + y * 4 + xx],
                dp,
                et_at(yy, x),
            )
            cp.start()
            first.append(cp)

    p_col = pm[:, lg_ref.shape[1] : lg_ref.shape[1] + 1]
    gate = g_ref[...].astype(F32)
    sig = jax.nn.sigmoid(gate)
    back_p = p_col * raw[:, 0:ff]
    gu_ref[...] = (back_p * gate * sig).astype(BF16)
    gg_ref[...] = (back_p * u_ref[...].astype(F32) * sig * (1.0 + gate * (1.0 - sig))).astype(BF16)

    def wg_wait(k, carry):
        src = et_at(y + k // 4, x + k % 4)
        arrived(wgb.at[src], wg_rs.at[src])
        return carry

    lax.fori_loop(1, 16, wg_wait, 0)
    wg = wgb[0]
    for k in range(1, 16):
        wg = wg + wgb[k]

    lgrad = (ct[0:16] * wg).astype(BF16)
    rpart = jnp.dot(lgrad, tslot[...], preferred_element_type=F32)
    rp[0] = rpart[0:8]
    rp[1] = rpart[8:16]
    mine = zp * 2 + c
    nears = []
    for k in (1, 2, 3):
        cp = copy(
            rp.at[(c + k) % 2], nearb.at[mine], near_ss.at[k], near_rs.at[mine], near_peer(k), et
        )
        cp.start()
        nears.append(cp)
    nearb[mine] = rp[c]
    for k in (1, 2, 3):
        src = ((zp + k // 2) % 2) * 2 + (c + k) % 2
        arrived(nearb.at[src], near_rs.at[src])
    total = ((nearb[0] + nearb[1]) + nearb[2]) + nearb[3]

    pieces = [total[:, k * 128 : (k + 1) * 128] for k in range(cols // 128)]
    pad = farb.shape[1] - 8 * len(pieces)
    farb[grp] = jnp.concatenate(pieces + [jnp.zeros((pad, 128), F32)], axis=0).astype(BF16)

    def far_copy(k):
        to = (((grp + k) % ngrp) * 2 + zp) * 2 + c
        return copy(farb.at[grp], farb.at[grp], far_ss.at[k], far_rs.at[grp], to, et)

    def far_send(i, carry):
        k = ngrp // 2 + (1 - 2 * (i % 2)) * ((i + 1) // 2)
        far_copy(k).start()
        return carry

    lax.fori_loop(0, ngrp - 1, far_send, 0)

    def row_sum(h, k):
        own = part[k * 4 + x, 0:half] if h == 0 else part[y * 4 + k, half:slots]
        acc = own.astype(F32)
        here = x if h == 0 else y
        for d in RING:
            src = (here + d) % 4
            arrived(r1.at[h, src, k], r1_rs.at[h * 16 + src * 4 + k])
            acc = acc + r1[h, src, k].astype(F32)
        return acc

    second = []
    for d in (2, 1, 3):
        for h in (0, 1):
            here = y if h == 0 else x
            k = (here + d) % 4
            p2[h, d] = row_sum(h, k).astype(BF16)
            to = et_at(k, x) if h == 0 else et_at(y, k)
            cp = copy(p2.at[h, d], r2.at[h, here], r2_ss.at[h * 4 + d], r2_rs.at[h * 4 + here], dp, to)
            cp.start()
            second.append(cp)

    def far_wait(k, carry):
        src = (grp + k) % ngrp
        arrived(farb.at[src], far_rs.at[src])
        return carry

    lax.fori_loop(1, ngrp, far_wait, 0)

    def far_add(k, acc):
        return acc + farb[k].astype(F32)

    total = lax.fori_loop(1, ngrp, far_add, farb[0].astype(F32)) * scale
    rgb[c] = jnp.concatenate([total[k * 8 : (k + 1) * 8] for k in range(cols // 128)], axis=1)
    swap = copy(rgb.at[c], rgb.at[c], core_ss, core_rs, near_peer(1), et)
    swap.start()

    out_rows = []
    for h in (0, 1):
        here = y if h == 0 else x
        acc = row_sum(h, here)
        for d in RING:
            src = (here + d) % 4
            arrived(r2.at[h, src], r2_rs.at[h * 4 + src])
            acc = acc + r2[h, src].astype(F32)
        out_rows.append(
            (acc * pm[h * half : (h + 1) * half, lg_ref.shape[1] : lg_ref.shape[1] + 1]).astype(BF16)
        )
    comb_ref[...] = lax.dot_general(
        onehot[...], jnp.concatenate(out_rows, axis=0), (((0,), (0,)), ((), ())), preferred_element_type=F32
    ).astype(BF16)

    arrived(rgb.at[1 - c], core_rs)
    rg_ref[0:8] = rgb[0]
    rg_ref[8:16] = rgb[1]

    for cp in sends + first + second + nears:
        cp.wait_send()

    def wg_done(k, carry):
        wg_copy(k).wait_send()
        return carry

    def far_done(k, carry):
        far_copy(k).wait_send()
        return carry

    lax.fori_loop(1, 16, wg_done, 0)
    lax.fori_loop(1, ngrp, far_done, 0)
    swap.wait_send()


def body(nz, pre_gate, pre_up, down_weight, row_token, block_count, router_logits, tokens_in, out_grad):
    slots, ff = pre_gate.shape
    toks, cols = tokens_in.shape
    half = slots // 2
    ffp = -(-ff // 128) * 128
    wide = down_weight.shape[1]
    ngrp = nz // 2
    experts = router_logits.shape[1]
    far_rows = -(-(8 * (cols // 128)) // 16) * 16
    scale = float((toks * nz * 2) ** -0.5)
    vmem = pl.BlockSpec(memory_space=pltpu.VMEM)
    dma = pltpu.SemaphoreType.DMA
    return pl.pallas_call(
        functools.partial(kernel, nz, scale),
        out_shape=(
            jax.ShapeDtypeStruct((toks, cols), BF16),
            jax.ShapeDtypeStruct((slots, ff), BF16),
            jax.ShapeDtypeStruct((slots, ff), BF16),
            jax.ShapeDtypeStruct((experts, cols), F32),
        ),
        in_specs=[
            vmem,
            pl.BlockSpec(memory_space=pltpu.SMEM),
            vmem,
            vmem,
            vmem,
            pl.BlockSpec(memory_space=pl.ANY),
            vmem,
            vmem,
        ],
        out_specs=(vmem, vmem, vmem, vmem),
        scratch_shapes=[
            pltpu.VMEM((ffp, wide), BF16),
            pltpu.VMEM((slots, ffp), BF16),
            pltpu.VMEM((toks, 128), F32),
            pltpu.VMEM((slots, toks), BF16),
            pltpu.VMEM((slots, 128), F32),
            pltpu.VMEM((128, slots), F32),
            pltpu.VMEM((slots, cols), BF16),
            pltpu.VMEM((16, slots, cols), BF16),
            pltpu.VMEM((slots, ffp), F32),
            pltpu.VMEM((16, slots, cols), BF16),
            pltpu.VMEM((2, 4, 4, half, cols), BF16),
            pltpu.VMEM((2, 4, half, cols), BF16),
            pltpu.VMEM((2, 4, half, cols), BF16),
            pltpu.VMEM((16, 1, slots), F32),
            pltpu.VMEM((2, 8, cols), F32),
            pltpu.VMEM((4, 8, cols), F32),
            pltpu.VMEM((ngrp, far_rows, 128), BF16),
            pltpu.VMEM((2, 8, cols), F32),
            dma,
            dma((30,)),
            dma((32,)),
            dma((24,)),
            dma((32,)),
            dma((8,)),
            dma((8,)),
            dma((16,)),
            dma((16,)),
            dma((4,)),
            dma((4,)),
            dma((ngrp,)),
            dma((ngrp,)),
            dma,
            dma,
        ],
        compiler_params=pltpu.CompilerParams(
            collective_id=1, has_side_effects=True, vmem_limit_bytes=48 * 2**20
        ),
        cost_estimate=pl.CostEstimate(
            flops=4 * slots * ff * wide, bytes_accessed=2 * ff * wide, transcendentals=slots * ff
        ),
        name="expert_down",
    )(
        row_token.reshape(1, slots),
        block_count,
        router_logits,
        pre_gate,
        pre_up,
        down_weight,
        tokens_in,
        out_grad,
    )


def solution(mesh):
    in_specs = (
        P("dp", "et"),
        P("dp", "et"),
        P("et", None),
        P("dp"),
        P("dp"),
        P("dp", None),
        P("dp", "et"),
        P("dp", "et"),
    )
    out_specs = (P("dp", "et"), P("dp", "et"), P("dp", "et"), P(None, "et"))
    nz = mesh.shape["dp"] // 2
    return jax.shard_map(
        functools.partial(body, nz), mesh=mesh, in_specs=in_specs, out_specs=out_specs, check_vma=False
    )
```

```python
import functools

import jax
import jax.numpy as jnp
from jax import lax
from jax.experimental import pallas as pl
from jax.experimental.pallas import tpu as pltpu
from jax.sharding import PartitionSpec as P

BLOCK = 128
MESH = pl.DeviceIdType.MESH
RING = (1, 3, 2)
F32 = jnp.float32
BF16 = jnp.bfloat16


def kernel(
    nz,
    scale,
    rt_hbm,
    bc_ref,
    lg_hbm,
    g_hbm,
    u_hbm,
    w_hbm,
    t_hbm,
    og_hbm,
    comb_ref,
    gg_ref,
    gu_ref,
    rg_ref,
    rt,
    lg,
    gt,
    ut,
    wv,
    tv,
    og,
    hid_t,
    hid,
    onehot,
    pm,
    ct,
    tslot,
    sg,
    raw,
    part,
    r1,
    p2,
    r2,
    wgb,
    rp,
    nearb,
    farb,
    rgb,
    in_sem,
    ready,
    ag_ss,
    ag_rs,
    r1_ss,
    r1_rs,
    r2_ss,
    r2_rs,
    wg_ss,
    wg_rs,
    near_ss,
    near_rs,
    far_ss,
    far_rs,
    core_ss,
    core_rs,
):
    ff, slots = gt.shape
    half = slots // 2
    ffp = hid.shape[1]
    toks, cols = og.shape
    experts = lg.shape[0]
    ngrp = nz // 2
    dp = lax.axis_index("dp")
    et = lax.axis_index("et")
    x, y, z, c = et % 4, et // 4, dp // 2, dp % 2
    zp, grp = z % 2, z // 2

    def et_at(yy, xx):
        return (yy % 4) * 4 + xx % 4

    def copy(src, dst, ss, rs, d_dp, d_et):
        return pltpu.make_async_remote_copy(
            src_ref=src, dst_ref=dst, send_sem=ss, recv_sem=rs, device_id=(d_dp, d_et), device_id_type=MESH
        )

    def arrived(ref, rs):
        copy(ref, ref, rs, rs, dp, et_at(y, x + 1)).wait_recv()

    def near_peer(k):
        return (grp * 2 + (zp + k // 2) % 2) * 2 + (c + k) % 2

    loads = {}
    pairs = dict(
        rt=(rt_hbm, rt), og=(og_hbm, og), g=(g_hbm, gt), u=(u_hbm, ut),
        w=(w_hbm, wv.at[pl.ds(0, ff)]), lg=(lg_hbm, lg), t=(t_hbm, tv),
    )
    for i, (name, (src, dst)) in enumerate(pairs.items()):
        loads[name] = pltpu.make_async_copy(src, dst, in_sem.at[i])
        loads[name].start()

    barrier = pltpu.get_barrier_semaphore()

    def greet(sem, d_dp, d_et):
        pl.semaphore_signal(sem, 1, device_id=(d_dp, d_et), device_id_type=MESH)

    def greet_et(k, carry):
        greet(barrier, dp, et_at(y + k // 4, x + k % 4))
        return carry

    def line(k):
        return (((grp + ngrp + k) % ngrp) * 2 + zp) * 2 + c

    greet(barrier, line(1), et)
    greet(barrier, line(-1), et)
    lax.fori_loop(1, 16, greet_et, 0)
    for k in (1, 2, 3):
        greet(barrier, near_peer(k), et)

    steps = ngrp.bit_length() - 2

    def ready_signal(i):
        greet(ready.at[i], line(1 << i), et)
        greet(ready.at[i], line(-(1 << i)), et)

    def ready_wait(i):
        pl.semaphore_wait(ready.at[i], 2)

    loads["rt"].wait()
    row_tok = rt[...]
    slot_block = lax.broadcasted_iota(jnp.int32, row_tok.shape, 1) // BLOCK
    row_tok = jnp.where((slot_block < bc_ref[0]) & (row_tok < toks), row_tok, toks).astype(F32)
    live = row_tok < float(toks)
    row_tok = jnp.broadcast_to(row_tok, (128, slots)).T
    for k in range(toks // 128):
        lane = lax.broadcasted_iota(jnp.int32, (slots, 128), 1).astype(F32) + float(k * 128)
        onehot[:, k * 128 : (k + 1) * 128] = jnp.where(row_tok == lane, 1.0, 0.0).astype(BF16)
    loads["og"].wait()
    sg[et] = jnp.dot(onehot[...], og[...], preferred_element_type=F32).astype(BF16)

    pl.semaphore_wait(barrier, 2 + 15 + 3)

    sends = []

    def send(block, h, d_et):
        view = sg.at[block, pl.ds(h * half, half)]
        cp = copy(view, view, ag_ss.at[len(sends)], ag_rs.at[block * 2 + h], dp, d_et)
        cp.start()
        sends.append(cp)

    def wait_block(block, h):
        arrived(sg.at[block, pl.ds(h * half, half)], ag_rs.at[block * 2 + h])

    for d in RING:
        send(et, 0, et_at(y, x + d))
        send(et, 1, et_at(y + d, x))
    for d in RING:
        send(et, 0, et_at(y + d, x))
        send(et, 1, et_at(y, x + d))

    ready_signal(0)

    loads["g"].wait()
    loads["u"].wait()
    gate = gt[...].astype(F32)
    hidden = jnp.where(live, gate * jax.nn.sigmoid(gate) * ut[...].astype(F32), 0.0)
    hid_t[ff:ffp] = jnp.zeros((ffp - ff, slots), F32)
    hid_t[0:ff] = hidden
    hid[...] = hid_t[...].T.astype(BF16)
    wv[ff:ffp] = jnp.zeros((ffp - ff, wv.shape[1]), BF16)
    loads["w"].wait()

    def forward_block(j, carry):
        w_j = wv[:, pl.ds(pl.multiple_of(j * cols, 128), cols)]
        part[j] = jnp.dot(hid[...], w_j, preferred_element_type=F32).astype(BF16)
        return carry

    lax.fori_loop(0, 16, forward_block, 0)

    ready_wait(0)
    ready_signal(1)

    for d in RING:
        block = et_at(y, x + d)
        wait_block(block, 0)
        for e in RING:
            send(block, 0, et_at(y + e, x))
        block = et_at(y + d, x)
        wait_block(block, 1)
        for e in RING:
            send(block, 1, et_at(y, x + e))

    loads["lg"].wait()
    logit = lg[...]
    ex = jnp.exp(logit - jnp.max(logit, axis=0, keepdims=True))
    probs = ex / jnp.sum(ex, axis=0, keepdims=True)
    p0 = probs[0:1]
    first_row = lax.broadcasted_iota(jnp.int32, probs.shape, 0) == 0
    coef = p0 * (jnp.where(first_row, 1.0, 0.0) - probs)
    table = jnp.concatenate([coef, jnp.broadcast_to(p0, coef.shape)], axis=0)
    hi = table.astype(BF16)
    rest = table - hi.astype(F32)
    mid = rest.astype(BF16)
    low = (rest - mid.astype(F32)).astype(BF16)

    def to_slots(rows):
        return lax.dot_general(rows, onehot[...], (((1,), (1,)), ((), ())), preferred_element_type=F32)

    ct[...] = (to_slots(low) + to_slots(mid)) + to_slots(hi)
    pm[...] = jnp.broadcast_to(ct[experts : experts + 1], (128, slots)).T
    loads["t"].wait()
    tslot[...] = jnp.dot(onehot[...], tv[...], preferred_element_type=F32).astype(BF16)

    ready_wait(1)
    ready_signal(2)

    def back(block):
        w_j = wv[0:ff, pl.ds(pl.multiple_of(block * cols, 128), cols)]
        return lax.dot_general(w_j, sg[block], (((1,), (1,)), ((), ())), preferred_element_type=F32)

    raw[...] = back(et)
    order = [(0, 1), (1, 0), (0, 3), (3, 0), (0, 2), (2, 0)]
    order += [(1, 1), (1, 3), (3, 1), (3, 3), (1, 2), (2, 1), (3, 2), (2, 3), (2, 2)]
    for dy, dx in order:
        block = et_at(y + dy, x + dx)
        if dx == 0:
            wait_block(block, 0)
        elif dy == 0:
            wait_block(block, 1)
        else:
            wait_block(block, 0)
            wait_block(block, 1)
        raw[...] += back(block)

    prod = hid_t[0:ff].astype(BF16).astype(F32) * raw[...]
    wgb[et] = jnp.sum(prod, axis=0, keepdims=True)

    def wg_copy(k):
        return copy(wgb.at[et], wgb.at[et], wg_ss.at[k], wg_rs.at[et], dp, et_at(y + k // 4, x + k % 4))

    def wg_send(k, carry):
        wg_copy(k).start()
        return carry

    lax.fori_loop(1, 16, wg_send, 0)

    first = []
    for far_off in (2, 1, 3, 0):
        for d in RING:
            yy, xx = (y + far_off) % 4, (x + d) % 4
            cp = copy(
                part.at[yy * 4 + xx, pl.ds(0, half)],
                r1.at[0, x, yy],
                r1_ss.at[len(first)],
                r1_rs.at[x * 4 + yy],
                dp,
                et_at(y, xx),
            )
            cp.start()
            first.append(cp)
            yy, xx = (y + d) % 4, (x + far_off) % 4
            cp = copy(
                part.at[yy * 4 + xx, pl.ds(half, half)],
                r1.at[1, y, xx],
                r1_ss.at[len(first)],
                r1_rs.at[16 + y * 4 + xx],
                dp,
                et_at(yy, x),
            )
            cp.start()
            first.append(cp)

    gate = gt[...].astype(F32)
    sig = jax.nn.sigmoid(gate)
    back_p = ct[experts : experts + 1] * raw[...]
    gu_ref[...] = (back_p * gate * sig).astype(BF16)
    gg_ref[...] = (back_p * ut[...].astype(F32) * sig * (1.0 + gate * (1.0 - sig))).astype(BF16)

    def wg_wait(k, carry):
        src = et_at(y + k // 4, x + k % 4)
        arrived(wgb.at[src], wg_rs.at[src])
        return carry

    lax.fori_loop(1, 16, wg_wait, 0)
    wg = wgb[0]
    for k in range(1, 16):
        wg = wg + wgb[k]

    lgrad = (ct[0:experts] * wg).astype(BF16)
    rpart = jnp.dot(lgrad, tslot[...], preferred_element_type=F32)
    rp[0] = rpart[0:8]
    rp[1] = rpart[8:16]
    mine = zp * 2 + c
    nears = []
    for k in (1, 2, 3):
        cp = copy(
            rp.at[(c + k) % 2], nearb.at[mine], near_ss.at[k], near_rs.at[mine], near_peer(k), et
        )
        cp.start()
        nears.append(cp)
    nearb[mine] = rp[c]
    for k in (1, 2, 3):
        src = ((zp + k // 2) % 2) * 2 + (c + k) % 2
        arrived(nearb.at[src], near_rs.at[src])
    total = ((nearb[0] + nearb[1]) + nearb[2]) + nearb[3]

    pieces = [total[:, k * 128 : (k + 1) * 128] for k in range(cols // 128)]
    pad = farb.shape[1] - 8 * len(pieces)
    farb[grp] = jnp.concatenate(pieces + [jnp.zeros((pad, 128), F32)], axis=0).astype(BF16)

    def far_copy(k):
        return copy(farb.at[grp], farb.at[grp], far_ss.at[k], far_rs.at[grp], line(k), et)

    for i in range(2, steps):
        ready_wait(i)
        if i < steps - 1:
            ready_signal(i + 1)

    def far_send(i, carry):
        k = ngrp // 2 + (1 - 2 * (i % 2)) * ((i + 1) // 2)
        far_copy(k).start()
        return carry

    lax.fori_loop(0, ngrp - 1, far_send, 0)

    def row_sum(h, k):
        own = part[k * 4 + x, 0:half] if h == 0 else part[y * 4 + k, half:slots]
        acc = own.astype(F32)
        here = x if h == 0 else y
        for d in RING:
            src = (here + d) % 4
            arrived(r1.at[h, src, k], r1_rs.at[h * 16 + src * 4 + k])
            acc = acc + r1[h, src, k].astype(F32)
        return acc

    second = []
    for d in (2, 1, 3):
        for h in (0, 1):
            here = y if h == 0 else x
            k = (here + d) % 4
            p2[h, d] = row_sum(h, k).astype(BF16)
            to = et_at(k, x) if h == 0 else et_at(y, k)
            cp = copy(p2.at[h, d], r2.at[h, here], r2_ss.at[h * 4 + d], r2_rs.at[h * 4 + here], dp, to)
            cp.start()
            second.append(cp)

    def far_wait(k, carry):
        src = (grp + k) % ngrp
        arrived(farb.at[src], far_rs.at[src])
        return carry

    lax.fori_loop(1, ngrp, far_wait, 0)

    def far_add(k, acc):
        return acc + farb[k].astype(F32)

    total = lax.fori_loop(1, ngrp, far_add, farb[0].astype(F32)) * scale
    rgb[c] = jnp.concatenate([total[k * 8 : (k + 1) * 8] for k in range(cols // 128)], axis=1)
    swap = copy(rgb.at[c], rgb.at[c], core_ss, core_rs, near_peer(1), et)
    swap.start()

    out_rows = []
    for h in (0, 1):
        here = y if h == 0 else x
        acc = row_sum(h, here)
        for d in RING:
            src = (here + d) % 4
            arrived(r2.at[h, src], r2_rs.at[h * 4 + src])
            acc = acc + r2[h, src].astype(F32)
        out_rows.append(
            (acc * pm[h * half : (h + 1) * half, 0:1]).astype(BF16)
        )
    comb_ref[...] = lax.dot_general(
        onehot[...], jnp.concatenate(out_rows, axis=0), (((0,), (0,)), ((), ())), preferred_element_type=F32
    ).astype(BF16)

    arrived(rgb.at[1 - c], core_rs)
    rg_ref[0:8] = rgb[0]
    rg_ref[8:16] = rgb[1]

    for cp in sends + first + second + nears:
        cp.wait_send()

    def wg_done(k, carry):
        wg_copy(k).wait_send()
        return carry

    def far_done(k, carry):
        far_copy(k).wait_send()
        return carry

    lax.fori_loop(1, 16, wg_done, 0)
    lax.fori_loop(1, ngrp, far_done, 0)
    swap.wait_send()


def finish(*refs):
    n = len(refs) // 2
    sems = refs[-1]
    copies = [pltpu.make_async_copy(refs[i], refs[n + i], sems.at[i]) for i in range(n)]
    for cp in copies:
        cp.start()
    for cp in copies:
        cp.wait()


def body(nz, pre_gate, pre_up, down_weight, row_token, block_count, router_logits, tokens_in, out_grad):
    slots, ff = pre_gate.shape
    toks, cols = tokens_in.shape
    half = slots // 2
    ffp = -(-ff // 128) * 128
    wide = down_weight.shape[1]
    ngrp = nz // 2
    experts = router_logits.shape[1]
    far_rows = -(-(8 * (cols // 128)) // 16) * 16
    scale = float((toks * nz * 2) ** -0.5)
    vmem = pl.BlockSpec(memory_space=pltpu.VMEM)
    hbm = pl.BlockSpec(memory_space=pltpu.HBM)
    dma = pltpu.SemaphoreType.DMA
    shapes = (
        jax.ShapeDtypeStruct((toks, cols), BF16),
        jax.ShapeDtypeStruct((ff, slots), BF16),
        jax.ShapeDtypeStruct((ff, slots), BF16),
        jax.ShapeDtypeStruct((experts, cols), F32),
    )
    results = pl.pallas_call(
        functools.partial(kernel, nz, scale),
        out_shape=shapes,
        in_specs=[hbm, pl.BlockSpec(memory_space=pltpu.SMEM), hbm, hbm, hbm, hbm, hbm, hbm],
        out_specs=(vmem, vmem, vmem, vmem),
        scratch_shapes=[
            pltpu.VMEM((1, slots), jnp.int32),
            pltpu.VMEM((experts, toks), F32),
            pltpu.VMEM((ff, slots), BF16),
            pltpu.VMEM((ff, slots), BF16),
            pltpu.VMEM((ffp, wide), BF16),
            pltpu.VMEM((toks, cols), BF16),
            pltpu.VMEM((toks, cols), BF16),
            pltpu.VMEM((ffp, slots), F32),
            pltpu.VMEM((slots, ffp), BF16),
            pltpu.VMEM((slots, toks), BF16),
            pltpu.VMEM((slots, 128), F32),
            pltpu.VMEM((2 * experts, slots), F32),
            pltpu.VMEM((slots, cols), BF16),
            pltpu.VMEM((16, slots, cols), BF16),
            pltpu.VMEM((ff, slots), F32),
            pltpu.VMEM((16, slots, cols), BF16),
            pltpu.VMEM((2, 4, 4, half, cols), BF16),
            pltpu.VMEM((2, 4, half, cols), BF16),
            pltpu.VMEM((2, 4, half, cols), BF16),
            pltpu.VMEM((16, 1, slots), F32),
            pltpu.VMEM((2, 8, cols), F32),
            pltpu.VMEM((4, 8, cols), F32),
            pltpu.VMEM((ngrp, far_rows, 128), BF16),
            pltpu.VMEM((2, 8, cols), F32),
            dma((7,)),
            pltpu.SemaphoreType.REGULAR((8,)),
            dma((30,)),
            dma((32,)),
            dma((24,)),
            dma((32,)),
            dma((8,)),
            dma((8,)),
            dma((16,)),
            dma((16,)),
            dma((4,)),
            dma((4,)),
            dma((ngrp,)),
            dma((ngrp,)),
            dma,
            dma,
        ],
        compiler_params=pltpu.CompilerParams(
            collective_id=1, has_side_effects=True, vmem_limit_bytes=62 * 2**20
        ),
        cost_estimate=pl.CostEstimate(
            flops=4 * slots * ff * wide, bytes_accessed=2 * ff * wide, transcendentals=slots * ff
        ),
        name="expert_down",
    )(
        row_token.reshape(1, slots),
        block_count,
        router_logits.T,
        pre_gate.T,
        pre_up.T,
        down_weight,
        tokens_in,
        out_grad,
    )
    combined, grad_gate, grad_up, router_grad = pl.pallas_call(
        finish,
        out_shape=shapes,
        in_specs=[hbm] * len(shapes),
        out_specs=(hbm,) * len(shapes),
        scratch_shapes=[dma((len(shapes),))],
        compiler_params=pltpu.CompilerParams(vmem_limit_bytes=62 * 2**20),
        name="write_results",
    )(*results)
    return combined, grad_gate.T, grad_up.T, router_grad


def solution(mesh):
    in_specs = (
        P("dp", "et"),
        P("dp", "et"),
        P("et", None),
        P("dp"),
        P("dp"),
        P("dp", None),
        P("dp", "et"),
        P("dp", "et"),
    )
    out_specs = (P("dp", "et"), P("dp", "et"), P("dp", "et"), P(None, "et"))
    nz = mesh.shape["dp"] // 2
    return jax.shard_map(
        functools.partial(body, nz), mesh=mesh, in_specs=in_specs, out_specs=out_specs, check_vma=False
    )
```

```python
import functools

import jax
import jax.numpy as jnp
from jax import lax
from jax.experimental import pallas as pl
from jax.experimental.pallas import tpu as pltpu
from jax.sharding import PartitionSpec as P

BLOCK = 128
MESH = pl.DeviceIdType.MESH
RING = (1, 3, 2)
NEXT = (1, 3)
EARLY = 0
F32 = jnp.float32
BF16 = jnp.bfloat16


def kernel(
    nz,
    scale,
    rt_hbm,
    bc_ref,
    lg_hbm,
    g_hbm,
    u_hbm,
    w_hbm,
    t_hbm,
    og_hbm,
    comb_ref,
    gg_ref,
    gu_ref,
    rg_ref,
    rt,
    lg,
    gt,
    ut,
    wv,
    tv,
    og,
    hid_t,
    hid,
    onehot,
    pm,
    ct,
    tslot,
    sg,
    raw,
    part,
    r1,
    p2,
    r2,
    wgb,
    rp,
    nearb,
    farb,
    rgb,
    gu,
    gg,
    comb,
    in_sem,
    out_sem,
    ready,
    ag_ss,
    ag_rs,
    r1_ss,
    r1_rs,
    r2_ss,
    r2_rs,
    wg_ss,
    wg_rs,
    near_ss,
    near_rs,
    far_ss,
    far_rs,
    core_ss,
    core_rs,
):
    ff, slots = gt.shape
    half = slots // 2
    ffp = hid.shape[1]
    toks, cols = og.shape
    experts = lg.shape[0]
    ngrp = nz // 2
    dp = lax.axis_index("dp")
    et = lax.axis_index("et")
    x, y, z, c = et % 4, et // 4, dp // 2, dp % 2
    zp, grp = z % 2, z // 2

    def et_at(yy, xx):
        return (yy % 4) * 4 + xx % 4

    def copy(src, dst, ss, rs, d_dp, d_et):
        return pltpu.make_async_remote_copy(
            src_ref=src, dst_ref=dst, send_sem=ss, recv_sem=rs, device_id=(d_dp, d_et), device_id_type=MESH
        )

    def arrived(ref, rs):
        copy(ref, ref, rs, rs, dp, et_at(y, x + 1)).wait_recv()

    def near_peer(k):
        return (grp * 2 + (zp + k // 2) % 2) * 2 + (c + k) % 2

    loads = {}
    pairs = dict(
        rt=(rt_hbm, rt), og=(og_hbm, og), g=(g_hbm, gt), u=(u_hbm, ut),
        w=(w_hbm, wv.at[pl.ds(0, ff)]), lg=(lg_hbm, lg), t=(t_hbm, tv),
    )
    for i, (name, (src, dst)) in enumerate(pairs.items()):
        loads[name] = pltpu.make_async_copy(src, dst, in_sem.at[i])
        loads[name].start()

    barrier = pltpu.get_barrier_semaphore()

    def greet(sem, d_dp, d_et):
        pl.semaphore_signal(sem, 1, device_id=(d_dp, d_et), device_id_type=MESH)

    def line(k):
        return (((grp + ngrp + k) % ngrp) * 2 + zp) * 2 + c

    for d in RING:
        greet(barrier, dp, et_at(y, x + d))
        greet(barrier, dp, et_at(y + d, x))
    greet(barrier, line(1), et)
    greet(barrier, line(-1), et)
    for k in (1, 2, 3):
        greet(barrier, near_peer(k), et)

    steps = ngrp.bit_length() - 2

    def ready_signal(i):
        greet(ready.at[i], line(1 << i), et)
        greet(ready.at[i], line(-(1 << i)), et)

    def ready_wait(i):
        pl.semaphore_wait(ready.at[i], 2)

    loads["rt"].wait()
    row_tok = rt[...]
    slot_block = lax.broadcasted_iota(jnp.int32, row_tok.shape, 1) // BLOCK
    row_tok = jnp.where((slot_block < bc_ref[0]) & (row_tok < toks), row_tok, toks).astype(F32)
    live = row_tok < float(toks)
    row_tok = jnp.broadcast_to(row_tok, (128, slots)).T
    for k in range(toks // 128):
        lane = lax.broadcasted_iota(jnp.int32, (slots, 128), 1).astype(F32) + float(k * 128)
        onehot[:, k * 128 : (k + 1) * 128] = jnp.where(row_tok == lane, 1.0, 0.0).astype(BF16)
    loads["og"].wait()
    sg[et] = jnp.dot(onehot[...], og[...], preferred_element_type=F32).astype(BF16)

    pl.semaphore_wait(barrier, 6 + 2 + 3)

    sends = []
    quart = half // 2

    def rows(block, h, q):
        if q is None:
            return sg.at[block, pl.ds(h * half, half)]
        return sg.at[block, pl.ds(h * half + q * quart, quart)]

    def send(block, h, d_et, q=None):
        view = rows(block, h, q)
        cp = copy(view, view, ag_ss.at[len(sends)], ag_rs.at[(block * 2 + h) * 2 + (q or 0)], dp, d_et)
        cp.start()
        sends.append(cp)

    def wait_block(block, h, q=None):
        arrived(rows(block, h, q), ag_rs.at[(block * 2 + h) * 2 + (q or 0)])

    for d in RING:
        send(et, 0, et_at(y, x + d))
        send(et, 1, et_at(y + d, x))
    for d in NEXT:
        send(et, 0, et_at(y + d, x))
        send(et, 1, et_at(y, x + d))

    ready_signal(0)

    loads["g"].wait()
    loads["u"].wait()
    gate = gt[...].astype(F32)
    hidden = jnp.where(live, gate * jax.nn.sigmoid(gate) * ut[...].astype(F32), 0.0)
    hid_t[ff:ffp] = jnp.zeros((ffp - ff, slots), F32)
    hid_t[0:ff] = hidden
    hid[...] = hid_t[...].T.astype(BF16)
    wv[ff:ffp] = jnp.zeros((ffp - ff, wv.shape[1]), BF16)

    def forward_block(j, carry):
        w_j = wv[:, pl.ds(pl.multiple_of(j * cols, 128), cols)]
        part[j] = jnp.dot(hid[...], w_j, preferred_element_type=F32).astype(BF16)
        return carry

    loads["w"].wait()
    lax.fori_loop(0, 4, forward_block, 0)

    for i, d in enumerate(RING):
        block = et_at(y, x + d)
        wait_block(block, 0)
        for e in NEXT:
            send(block, 0, et_at(y + e, x))
        block = et_at(y + d, x)
        wait_block(block, 1)
        for e in NEXT:
            send(block, 1, et_at(y, x + e))
        lax.fori_loop(4 * i + 4, 4 * i + 8, forward_block, 0)

    ready_wait(0)
    ready_signal(1)

    loads["lg"].wait()
    logit = lg[...]
    ex = jnp.exp(logit - jnp.max(logit, axis=0, keepdims=True))
    probs = ex / jnp.sum(ex, axis=0, keepdims=True)
    p0 = probs[0:1]
    first_row = lax.broadcasted_iota(jnp.int32, probs.shape, 0) == 0
    coef = p0 * (jnp.where(first_row, 1.0, 0.0) - probs)
    table = jnp.concatenate([coef, jnp.broadcast_to(p0, coef.shape)], axis=0)
    hi = table.astype(BF16)
    rest = table - hi.astype(F32)
    mid = rest.astype(BF16)
    low = (rest - mid.astype(F32)).astype(BF16)

    def to_slots(rows):
        return lax.dot_general(rows, onehot[...], (((1,), (1,)), ((), ())), preferred_element_type=F32)

    ct[...] = (to_slots(low) + to_slots(mid)) + to_slots(hi)
    pm[...] = jnp.broadcast_to(ct[experts : experts + 1], (128, slots)).T
    loads["t"].wait()
    tslot[...] = jnp.dot(onehot[...], tv[...], preferred_element_type=F32).astype(BF16)

    def back(block):
        w_j = wv[0:ff, pl.ds(pl.multiple_of(block * cols, 128), cols)]
        return lax.dot_general(w_j, sg[block], (((1,), (1,)), ((), ())), preferred_element_type=F32)

    def add_back(dy, dx):
        raw[...] += back(et_at(y + dy, x + dx))

    first = []

    def scatter(far_off, d):
        yy, xx = (y + far_off) % 4, (x + d) % 4
        first.append(
            copy(
                part.at[yy * 4 + xx, pl.ds(0, half)],
                r1.at[0, x, yy],
                r1_ss.at[len(first)],
                r1_rs.at[x * 4 + yy],
                dp,
                et_at(y, xx),
            )
        )
        first[-1].start()
        yy, xx = (y + d) % 4, (x + far_off) % 4
        first.append(
            copy(
                part.at[yy * 4 + xx, pl.ds(half, half)],
                r1.at[1, y, xx],
                r1_ss.at[len(first)],
                r1_rs.at[16 + y * 4 + xx],
                dp,
                et_at(yy, x),
            )
        )
        first[-1].start()

    scatters = [(far_off, d) for far_off in (2, 1, 3, 0) for d in RING]

    raw[...] = back(et)
    whole = {0: [(1, 0), (3, 0), (0, 1), (0, 3)], 1: [(1, 1)], 3: [(1, 3), (3, 1), (3, 3)], 2: []}
    for d in (0,) + RING:
        for e in NEXT:
            q = 1 if e == 1 else 0
            block = et_at(y + e, x + d)
            wait_block(block, 0)
            send(block, 0, et_at(y + 4 - e, x), q)
            block = et_at(y + d, x + e)
            wait_block(block, 1)
            send(block, 1, et_at(y, x + 4 - e), q)
        for pair in whole[d]:
            add_back(*pair)
    ready_wait(1)
    ready_signal(2)
    for pair in scatters[:EARLY]:
        scatter(*pair)
    for d in (0,) + RING:
        for q in (0, 1):
            wait_block(et_at(y + 2, x + d), 0, q)
            wait_block(et_at(y + d, x + 2), 1, q)
        add_back(2, d)
        if d != 2:
            add_back(d, 2)

    prod = hid_t[0:ff].astype(BF16).astype(F32) * raw[...]
    wgb[et] = jnp.sum(prod, axis=0, keepdims=True)

    def wg_copy(k):
        return copy(wgb.at[et], wgb.at[et], wg_ss.at[k], wg_rs.at[et], dp, et_at(y + k // 4, x + k % 4))

    def wg_send(k, carry):
        wg_copy(k).start()
        return carry

    lax.fori_loop(1, 16, wg_send, 0)

    for pair in scatters[EARLY:]:
        scatter(*pair)

    gate = gt[...].astype(F32)
    sig = jax.nn.sigmoid(gate)
    back_p = ct[experts : experts + 1] * raw[...]
    gu[...] = (back_p * gate * sig).astype(BF16)
    gg[...] = (back_p * ut[...].astype(F32) * sig * (1.0 + gate * (1.0 - sig))).astype(BF16)
    stores = [
        pltpu.make_async_copy(gu, gu_ref, out_sem.at[0]),
        pltpu.make_async_copy(gg, gg_ref, out_sem.at[1]),
    ]
    for cp in stores:
        cp.start()

    def wg_wait(k, carry):
        src = et_at(y + k // 4, x + k % 4)
        arrived(wgb.at[src], wg_rs.at[src])
        return carry

    lax.fori_loop(1, 16, wg_wait, 0)
    wg = wgb[0]
    for k in range(1, 16):
        wg = wg + wgb[k]

    lgrad = (ct[0:experts] * wg).astype(BF16)
    rpart = jnp.dot(lgrad, tslot[...], preferred_element_type=F32)
    quarters = range(4)
    chunks = range(cols // 128)
    each = experts // 4
    empty = jnp.zeros((rp.shape[1] - each * len(chunks), 128), F32)
    for q in quarters:
        own_rows = rpart[q * each : (q + 1) * each]
        rp[q] = jnp.concatenate([own_rows[:, k * 128 : (k + 1) * 128] for k in chunks] + [empty], axis=0)
    mine = zp * 2 + c
    nears = []

    def quarter_of(k):
        return ((zp + k // 2) % 2) * 2 + (c + k) % 2

    for k in (1, 2, 3):
        cp = copy(rp.at[quarter_of(k)], nearb.at[mine], near_ss.at[k], near_rs.at[mine], near_peer(k), et)
        cp.start()
        nears.append(cp)
    nearb[mine] = rp[mine]
    for k in (1, 2, 3):
        src = quarter_of(k)
        arrived(nearb.at[src], near_rs.at[src])
    total = ((nearb[0] + nearb[1]) + nearb[2]) + nearb[3]

    farb[grp] = total.astype(BF16)

    def far_copy(k):
        return copy(farb.at[grp], farb.at[grp], far_ss.at[k], far_rs.at[grp], line(k), et)

    for i in range(2, steps):
        ready_wait(i)
        if i < steps - 1:
            ready_signal(i + 1)

    def far_send(i, carry):
        k = ngrp // 2 + (1 - 2 * (i % 2)) * ((i + 1) // 2)
        far_copy(k).start()
        return carry

    lax.fori_loop(0, ngrp - 1, far_send, 0)

    def row_sum(h, k):
        own = part[k * 4 + x, 0:half] if h == 0 else part[y * 4 + k, half:slots]
        acc = own.astype(F32)
        here = x if h == 0 else y
        for d in RING:
            src = (here + d) % 4
            arrived(r1.at[h, src, k], r1_rs.at[h * 16 + src * 4 + k])
            acc = acc + r1[h, src, k].astype(F32)
        return acc

    second = []
    for d in (2, 1, 3):
        for h in (0, 1):
            here = y if h == 0 else x
            k = (here + d) % 4
            p2[h, d] = row_sum(h, k).astype(BF16)
            to = et_at(k, x) if h == 0 else et_at(y, k)
            cp = copy(p2.at[h, d], r2.at[h, here], r2_ss.at[h * 4 + d], r2_rs.at[h * 4 + here], dp, to)
            cp.start()
            second.append(cp)

    def far_wait(k, carry):
        src = (grp + k) % ngrp
        arrived(farb.at[src], far_rs.at[src])
        return carry

    lax.fori_loop(1, ngrp, far_wait, 0)

    def far_add(k, acc):
        return acc + farb[k].astype(F32)

    total = lax.fori_loop(1, ngrp, far_add, farb[0].astype(F32)) * scale
    rgb[...] = total
    for k in (1, 2, 3):
        cp = copy(rgb, rg_ref.at[mine], core_ss.at[k], core_rs.at[mine], near_peer(k), et)
        cp.start()
        nears.append(cp)
    stores.append(pltpu.make_async_copy(rgb, rg_ref.at[mine], out_sem.at[2]))
    stores[-1].start()

    out_rows = []
    for h in (0, 1):
        here = y if h == 0 else x
        acc = row_sum(h, here)
        for d in RING:
            src = (here + d) % 4
            arrived(r2.at[h, src], r2_rs.at[h * 4 + src])
            acc = acc + r2[h, src].astype(F32)
        out_rows.append(
            (acc * pm[h * half : (h + 1) * half, 0:1]).astype(BF16)
        )
    comb[...] = lax.dot_general(
        onehot[...], jnp.concatenate(out_rows, axis=0), (((0,), (0,)), ((), ())), preferred_element_type=F32
    ).astype(BF16)

    stores.append(pltpu.make_async_copy(comb, comb_ref, out_sem.at[3]))
    stores[-1].start()
    for k in (1, 2, 3):
        src = quarter_of(k)
        arrived(rg_ref.at[src], core_rs.at[src])
    for cp in stores:
        cp.wait()

    for cp in sends + first + second + nears:
        cp.wait_send()

    def wg_done(k, carry):
        wg_copy(k).wait_send()
        return carry

    def far_done(k, carry):
        far_copy(k).wait_send()
        return carry

    lax.fori_loop(1, 16, wg_done, 0)
    lax.fori_loop(1, ngrp, far_done, 0)


def finish(n, *refs):
    held, rows, in_sem, out_sem = refs[2 * n : 3 * n], refs[3 * n], refs[3 * n + 1], refs[3 * n + 2]
    ins = [pltpu.make_async_copy(refs[i], held[i], in_sem.at[i]) for i in range(n)]
    outs = [pltpu.make_async_copy(held[i] if i < n - 1 else rows, refs[n + i], out_sem.at[i]) for i in range(n)]
    for cp in ins:
        cp.start()
    for cp, out in zip(ins[:-1], outs[:-1]):
        cp.wait()
        out.start()
    ins[-1].wait()
    each = rows.shape[0] // 4
    for q in range(4):
        for k in range(rows.shape[1] // 128):
            piece = held[-1][q, k * each : (k + 1) * each]
            rows[q * each : (q + 1) * each, k * 128 : (k + 1) * 128] = piece
    outs[-1].start()
    for cp in outs:
        cp.wait()


def body(nz, pre_gate, pre_up, down_weight, row_token, block_count, router_logits, tokens_in, out_grad):
    slots, ff = pre_gate.shape
    toks, cols = tokens_in.shape
    half = slots // 2
    ffp = -(-ff // 128) * 128
    wide = down_weight.shape[1]
    ngrp = nz // 2
    experts = router_logits.shape[1]
    far_rows = -(-(experts // 4 * (cols // 128)) // 16) * 16
    scale = float((toks * nz * 2) ** -0.5)
    hbm = pl.BlockSpec(memory_space=pltpu.HBM)
    dma = pltpu.SemaphoreType.DMA
    shapes = (
        jax.ShapeDtypeStruct((toks, cols), BF16),
        jax.ShapeDtypeStruct((ff, slots), BF16),
        jax.ShapeDtypeStruct((ff, slots), BF16),
        jax.ShapeDtypeStruct((4, far_rows, 128), F32),
    )
    results = pl.pallas_call(
        functools.partial(kernel, nz, scale),
        out_shape=shapes,
        in_specs=[hbm, pl.BlockSpec(memory_space=pltpu.SMEM), hbm, hbm, hbm, hbm, hbm, hbm],
        out_specs=(hbm,) * len(shapes),
        scratch_shapes=[
            pltpu.VMEM((1, slots), jnp.int32),
            pltpu.VMEM((experts, toks), F32),
            pltpu.VMEM((ff, slots), BF16),
            pltpu.VMEM((ff, slots), BF16),
            pltpu.VMEM((ffp, wide), BF16),
            pltpu.VMEM((toks, cols), BF16),
            pltpu.VMEM((toks, cols), BF16),
            pltpu.VMEM((ffp, slots), F32),
            pltpu.VMEM((slots, ffp), BF16),
            pltpu.VMEM((slots, toks), BF16),
            pltpu.VMEM((slots, 128), F32),
            pltpu.VMEM((2 * experts, slots), F32),
            pltpu.VMEM((slots, cols), BF16),
            pltpu.VMEM((16, slots, cols), BF16),
            pltpu.VMEM((ff, slots), F32),
            pltpu.VMEM((16, slots, cols), BF16),
            pltpu.VMEM((2, 4, 4, half, cols), BF16),
            pltpu.VMEM((2, 4, half, cols), BF16),
            pltpu.VMEM((2, 4, half, cols), BF16),
            pltpu.VMEM((16, 1, slots), F32),
            pltpu.VMEM((4, far_rows, 128), F32),
            pltpu.VMEM((4, far_rows, 128), F32),
            pltpu.VMEM((ngrp, far_rows, 128), BF16),
            pltpu.VMEM((far_rows, 128), F32),
            pltpu.VMEM((ff, slots), BF16),
            pltpu.VMEM((ff, slots), BF16),
            pltpu.VMEM((toks, cols), BF16),
            dma((7,)),
            dma((4,)),
            pltpu.SemaphoreType.REGULAR((8,)),
            dma((38,)),
            dma((64,)),
            dma((24,)),
            dma((32,)),
            dma((8,)),
            dma((8,)),
            dma((16,)),
            dma((16,)),
            dma((4,)),
            dma((4,)),
            dma((ngrp,)),
            dma((ngrp,)),
            dma((4,)),
            dma((4,)),
        ],
        compiler_params=pltpu.CompilerParams(
            collective_id=1, has_side_effects=True, vmem_limit_bytes=62 * 2**20
        ),
        cost_estimate=pl.CostEstimate(
            flops=4 * slots * ff * wide, bytes_accessed=2 * ff * wide, transcendentals=slots * ff
        ),
        name="expert_down",
    )(
        row_token.reshape(1, slots),
        block_count,
        router_logits.T,
        pre_gate.T,
        pre_up.T,
        down_weight,
        tokens_in,
        out_grad,
    )
    combined, grad_gate, grad_up, router_grad = pl.pallas_call(
        functools.partial(finish, len(shapes)),
        out_shape=shapes[:-1] + (jax.ShapeDtypeStruct((experts, cols), F32),),
        in_specs=[hbm] * len(shapes),
        out_specs=(hbm,) * len(shapes),
        scratch_shapes=[pltpu.VMEM(a.shape, a.dtype) for a in shapes]
        + [pltpu.VMEM((experts, cols), F32), dma((len(shapes),)), dma((len(shapes),))],
        compiler_params=pltpu.CompilerParams(vmem_limit_bytes=62 * 2**20),
        name="write_results",
    )(*results)
    return combined, grad_gate.T, grad_up.T, router_grad


def solution(mesh):
    in_specs = (
        P("dp", "et"),
        P("dp", "et"),
        P("et", None),
        P("dp"),
        P("dp"),
        P("dp", None),
        P("dp", "et"),
        P("dp", "et"),
    )
    out_specs = (P("dp", "et"), P("dp", "et"), P("dp", "et"), P(None, "et"))
    nz = mesh.shape["dp"] // 2
    return jax.shard_map(
        functools.partial(body, nz), mesh=mesh, in_specs=in_specs, out_specs=out_specs, check_vma=False
    )
```
